1024 devices in a mesh: code: 64 (over x_hi, y, core), dp: 16 (over x_lo, z).
Axes of the slice: x: 8 (x_hi: 4, x_lo: 2; x = x_hi * 2 + x_lo), y: 8, z: 8, core: 2. Of those that a mesh axis runs over, the one named last changes fastest.
Arguments:
- cold_table: float32 [64, 16, 4, 512, 128], P('code', 'dp'), may hold values from -6 to 6
- block_ids: int32 [64, 16, 4], P('code', 'dp'), may hold values from 0 to 3
- counts: int32 [64, 16], P('code', 'dp'), may hold values from 1 to 4
- group_map: int32 [64], P('code'), may hold values from 0 to 7, as said below
- coef: float32 [2, 8], replicated, may hold values from 0.5 to 2
- batch_ids: int32 [64, 16, 1024], P('code', 'dp'), may hold values from 0 to 2047
- out_grad: float32 [64, 16, 1024, 128], P('code', 'dp'), may hold values from -6 to 6
- hot_weights: float32 [2048, 128], replicated, may hold values from -6 to 6
- accum: float32 [2048], replicated, may hold values from 0.01 to 1
Outputs:
- parity_shards: float32 [64, 16, 2, 4, 64, 128], P('code', 'dp')
- new_weights: float32 [2048, 128], replicated
- new_accum: float32 [2048], replicated
The draws below stay inside these ranges and needn't reach their ends.
Inputs may be any that keep to these rules, and one draw needn't show every extreme that they name: `group_map`: each aligned run of 8 code positions holds each of 0 to 7 once.
All inputs are finite; a program needn't handle non-finite values.
Results may differ from the reference program's by a relative error of at most 0.0003.
Values sent between devices are 32-bit elements; how exact they have to be, the bound alone decides.
No kernel may reach another device: no remote copies, remote signals or barrier semaphores. Data moves between devices by JAX's collectives and lax.ppermute only.
A program may use at most 32 MiB of HBM per device.

```python
import math
import jax
import jax.numpy as jnp
import numpy as np
from jax import lax

E = 128
BR = 512
CB = 4
SLOTS = 4
HOT = 2048
B_DEV = 1024
GROUPS = 8
REPLICAS = 16


def draw_group_map(key, part):
    key = jax.random.fold_in(key, 7)
    keys = jax.random.split(key, GROUPS)
    orders = jax.vmap(lambda single: jax.random.permutation(single, 8))(keys)
    return orders.reshape(GROUPS * 8).astype(jnp.int32)


def place_ends(array, rng, smallest, largest):
    place = [jax.random.randint(jax.random.fold_in(rng, axis), (), 0, length) for axis, length in enumerate(array.shape)]
    main_axis = array.shape.index(max(array.shape))
    beside = place[:main_axis] + [(place[main_axis] + 1) % array.shape[main_axis]] + place[main_axis + 1:]
    return array.at[tuple(place)].set(smallest).at[tuple(beside)].set(largest)


def steps_of(key, extent, cuts, smallest, largest):
    gain, own = 1.0, jax.random.fold_in(key, 6)
    for dim, parts in cuts:
        draws = jnp.exp(jax.random.uniform(jax.random.fold_in(own, dim), (parts,), jnp.float32, smallest / len(cuts), largest / len(cuts)))
        gain = gain * jnp.repeat(draws, extent[dim] // parts).reshape([-1 if axis == dim else 1 for axis in range(len(extent))])
    return gain


def rank_table(amount, slope):
    loads = [(1 << 20) // math.isqrt(rank ** slope) + 1 for rank in range(1, amount + 1)]
    scale = 1 + sum(loads) // (1 << 30)
    return np.cumsum(np.array([max(1, weight // scale) for weight in loads]))


def ranked_ids(own_key, shape, count, lean):
    grid = rank_table(count, lean)
    pick = jax.random.randint(jax.random.fold_in(own_key, 1), shape, 0, int(grid[count - 1]))
    rank = jnp.searchsorted(jnp.asarray(grid, jnp.int32), pick, side="right")
    return jax.random.permutation(jax.random.fold_in(own_key, 2), count)[rank].astype(jnp.int32)


def centred(own_key, dims, spread, most, cuts=(), dtype=jnp.bfloat16):
    array = jax.random.normal(own_key, dims, jnp.float32) * spread
    if len(cuts) > 0:
        array = steps_of(own_key, dims, cuts, -0.22, 0.18) * array
    return jnp.clip(array, min=-most, max=most).astype(dtype)


def setup_inputs(seed: int = 0) -> dict:
    key_of = jax.random.split(jax.random.key(seed), 10)
    cold_table = centred(key_of[0], (GROUPS * 8, REPLICAS, CB, BR, E), 1.0, 6.0, ((0, 64), (1, 16)), jnp.float32)
    block_ids = place_ends(jax.random.randint(key_of[1], (GROUPS * 8, REPLICAS, SLOTS), 0, CB), jax.random.fold_in(key_of[1], 1), 0, CB - 1).astype(jnp.int32)
    counts = place_ends(jax.random.randint(key_of[2], (GROUPS * 8, REPLICAS), 1, SLOTS + 1), jax.random.fold_in(key_of[2], 1), 1, SLOTS).astype(jnp.int32)
    group_map = draw_group_map(jax.random.fold_in(key_of[9], 71), 0)
    coef = jnp.clip(jax.random.uniform(key_of[4], (2, 8), jnp.float32, 0.5, 2.0), 0.5, 2.0)
    batch_ids = place_ends(ranked_ids(key_of[5], (GROUPS * 8, REPLICAS, B_DEV), HOT, 2), jax.random.fold_in(key_of[5], 3), 0, HOT - 1).astype(jnp.int32)
    out_grad = centred(key_of[6], (GROUPS * 8, REPLICAS, B_DEV, E), 1.0, 6.0, ((0, 64), (1, 16)), jnp.float32)
    hot_weights = centred(key_of[7], (HOT, E), 1.0, 6.0, (), jnp.float32)
    accum = jnp.clip(jnp.exp(jax.random.uniform(key_of[8], (HOT,), jnp.float32, math.log(0.01), math.log(1.0))), 0.01, 1.0)
    return {"cold_table": cold_table, "block_ids": block_ids, "counts": counts, "group_map": group_map, "coef": coef, "batch_ids": batch_ids, "out_grad": out_grad, "hot_weights": hot_weights, "accum": accum}


def reference(cold_table, block_ids, counts, group_map, coef, batch_ids, out_grad, hot_weights, accum):
    tables = cold_table.reshape(GROUPS, 8, REPLICAS, CB, BR, E)
    ids_all = block_ids.reshape(GROUPS, 8, REPLICAS, SLOTS)
    live_all = counts.reshape(GROUPS, 8, REPLICAS)
    members_all = group_map.reshape(GROUPS, 8)

    def encode_group(inputs):
        group_tables, group_ids, group_counts, members = inputs
        chosen = jax.vmap(jax.vmap(lambda table, index: table[index]))(group_tables, group_ids)
        live = (jnp.arange(SLOTS)[None, None, :] < group_counts[:, :, None]).astype(jnp.float32)
        chosen = chosen * live[:, :, :, None, None]
        column = coef[:, members]
        parity = jnp.einsum('pm,mrsij->rpsij', column, chosen, precision=lax.Precision.HIGHEST)
        parity = parity.reshape(REPLICAS, 2, SLOTS, 8, BR // 8, E)
        return jnp.transpose(parity, (3, 0, 1, 2, 4, 5))
    parity_shards = lax.map(encode_group, (tables, ids_all, live_all, members_all))
    parity_shards = parity_shards.reshape(GROUPS * 8, REPLICAS, 2, SLOTS, BR // 8, E)
    grad = jax.ops.segment_sum(out_grad.reshape(-1, E), batch_ids.reshape(-1), num_segments=HOT)
    new_accum = accum + lax.optimization_barrier(jnp.mean(grad * grad, axis=1))
    new_weights = hot_weights - 0.5 * grad / (jnp.sqrt(new_accum)[:, None] + 1e-06)
    return (parity_shards, new_weights, new_accum)
```

```python
import jax
import jax.numpy as jnp
from jax import lax
from jax.sharding import Mesh, PartitionSpec as P

NAMES = ("xh", "xm", "yh", "ym", "yl", "core", "xl", "z")
SIZES = (2, 2, 2, 2, 2, 2, 2, 8)
CODE = ("xh", "xm", "yh", "ym", "yl", "core")
DP = ("xl", "z")
NEAR = ("xm", "xl", "z")
FAR = ("xh", "yh", "ym", "yl")


def size(axes):
    return lax.axis_size(axes)


def exchange(parts, axes):
    return lax.all_to_all(parts, axes, 0, 0, tiled=True)


def to_all(block, axes):
    return exchange(jnp.broadcast_to(block[None], (size(axes),) + block.shape), axes)


def swap(value, axis):
    return lax.ppermute(value, axis, [(0, 1), (1, 0)])


def pick(value, place, axis):
    return lax.dynamic_index_in_dim(value, place, axis, keepdims=False)


def adagrad(grad, weights, accumulators):
    updated_accum = accumulators + jnp.mean(grad * grad, axis=1)
    updated = weights - 0.5 * grad / (jnp.sqrt(updated_accum)[:, None] + 1e-06)
    return (updated, updated_accum)


def partial_grad(ids, rows_grad, first, rows):
    onehot = (ids[:, None] - first == jnp.arange(rows)[None, :]).astype(jnp.float32)
    return lax.dot_general(
        onehot,
        rows_grad,
        (((0,), (0,)), ((), ())),
        precision=lax.Precision.HIGHEST,
        preferred_element_type=jnp.float32,
    )


def shards(cold_table, block_ids, counts, group_map, coef, batch_ids, out_grad, hot_weights, accum):
    slot_count = block_ids.shape[2]
    block_rows = cold_table.shape[3]
    width = cold_table.shape[4]
    hot_rows = hot_weights.shape[0]
    part_rows = block_rows // 8
    core = lax.axis_index("core")

    live = (jnp.arange(slot_count) < counts[0, 0]).astype(jnp.float32)
    masked = cold_table[0, 0][block_ids[0, 0]] * live[:, None, None]
    column = coef[:, group_map[0]]
    masked = masked.reshape(slot_count, 4, 2, part_rows, width)
    parity = column[:, None, None, None, None] * pick(masked, core, 2)[None]
    away = column[:, None, None, None, None] * pick(masked, 1 - core, 2)[None]
    parity = parity + swap(away, "core")
    for axis in ("yl", "ym"):
        place = lax.axis_index(axis)
        parity = parity.reshape(2, slot_count, -1, 2, part_rows, width) if axis == "yl" else parity
        parity = pick(parity, place, -3) + swap(pick(parity, 1 - place, -3), axis)
    parity_shards = parity[None, None]

    half = hot_rows // 2
    theirs = partial_grad(batch_ids[0, 0], out_grad[0, 0], (1 - core) * half, half)
    arrived = swap(theirs, "core")
    grad = partial_grad(batch_ids[0, 0], out_grad[0, 0], core * half, half) + arrived
    near = size(NEAR)
    grad = exchange(grad.reshape(near, half // near, width), NEAR).sum(axis=0)
    grad = to_all(grad, FAR).sum(axis=0)
    grad = to_all(grad, NEAR).reshape(half, width)
    other = swap(grad, "core")
    low, high = jnp.where(core == 0, grad, other), jnp.where(core == 0, other, grad)
    grad = jnp.concatenate([low, high], axis=0)
    new_weights, new_accum = adagrad(grad, hot_weights, accum)
    return (parity_shards, new_weights, new_accum)


def solution(mesh):
    mesh = Mesh(mesh.devices.reshape(SIZES), NAMES)
    in_specs = (
        P(CODE, DP, None, None, None),
        P(CODE, DP, None),
        P(CODE, DP),
        P(CODE),
        P(),
        P(CODE, DP, None),
        P(CODE, DP, None, None),
        P(),
        P(),
    )
    out_specs = (P(CODE, DP, None, None, None, None), P(), P())
    return jax.shard_map(shards, mesh=mesh, in_specs=in_specs, out_specs=out_specs, check_vma=False)
```

```python
import jax
import jax.numpy as jnp
from jax import lax
from jax.experimental import pallas as pl
from jax.experimental.pallas import tpu as pltpu
from jax.sharding import Mesh, PartitionSpec as P

NAMES = ("xh", "xm", "yh", "ym", "yl", "core", "xl", "z")
SIZES = (2, 2, 2, 2, 2, 2, 2, 8)
CODE = ("xh", "xm", "yh", "ym", "yl", "core")
DP = ("xl", "z")
NEAR = ("xm", "xl", "z")
TILE = 256
FAR = ("xh", "yh", "ym", "yl")


def size(axes):
    return lax.axis_size(axes)


def exchange(parts, axes):
    return lax.all_to_all(parts, axes, 0, 0, tiled=True)


def sum_copies_kernel(parts_ref, ready_ref, copies_ref):
    total = parts_ref[0]
    for part in range(1, parts_ref.shape[0]):
        total = total + parts_ref[part]
    copies_ref[...] = jnp.broadcast_to(total[None], copies_ref.shape)


def sum_copies(parts, copies, ready):
    shape = (copies,) + parts.shape[1:]
    return pl.pallas_call(
        sum_copies_kernel,
        out_shape=jax.ShapeDtypeStruct(shape, jnp.float32),
        in_specs=[pl.BlockSpec(memory_space=pltpu.VMEM), pl.BlockSpec(memory_space=pl.ANY)],
        out_specs=pl.BlockSpec(memory_space=pltpu.VMEM),
        cost_estimate=pl.CostEstimate(flops=parts.size, bytes_accessed=4 * parts.size, transcendentals=0),
        compiler_params=pltpu.CompilerParams(vmem_limit_bytes=24 << 20),
        name="sum_copies",
    )(parts, ready)


def swap(value, axis):
    return lax.ppermute(value, axis, [(0, 1), (1, 0)])


def pick(value, place, axis):
    return lax.dynamic_index_in_dim(value, place, axis, keepdims=False)


def sum_kernel(first_ref, ids_ref, rows_ref, out_ref):
    width = rows_ref.shape[1]
    value = rows_ref[...]
    high = value.astype(jnp.bfloat16)
    rest = value - high.astype(jnp.float32)
    middle = rest.astype(jnp.bfloat16)
    low = (rest - middle.astype(jnp.float32)).astype(jnp.bfloat16)
    three = jnp.concatenate([high, middle, low], axis=1)
    ids = ids_ref[...] - first_ref[0]
    for tile in range(out_ref.shape[0] // TILE):
        row = lax.broadcasted_iota(jnp.int32, (TILE, ids.shape[1]), 0) + tile * TILE
        hit = jnp.where(row == ids, 1.0, 0.0).astype(jnp.bfloat16)
        part = jnp.dot(hit, three, preferred_element_type=jnp.float32)
        total = part[:, :width] + part[:, width : 2 * width] + part[:, 2 * width :]
        out_ref[tile * TILE : (tile + 1) * TILE, :] = total


def partial_grad(ids, rows_grad, first, rows):
    lookups, width = rows_grad.shape
    return pl.pallas_call(
        sum_kernel,
        out_shape=jax.ShapeDtypeStruct((rows, width), jnp.float32),
        in_specs=[
            pl.BlockSpec(memory_space=pltpu.SMEM),
            pl.BlockSpec(memory_space=pltpu.VMEM),
            pl.BlockSpec(memory_space=pltpu.VMEM),
        ],
        out_specs=pl.BlockSpec(memory_space=pltpu.VMEM),
        cost_estimate=pl.CostEstimate(flops=6 * rows * lookups * width, bytes_accessed=4 * (lookups + rows) * width, transcendentals=0),
        compiler_params=pltpu.CompilerParams(vmem_limit_bytes=24 << 20),
        name="hot_rows_sum",
    )(first.reshape(1), ids.reshape(1, lookups), rows_grad)


def coded_kernel(ids_ref, counts_ref, column_ref, core_ref, coef_ref, cold_ref, ready_ref, kept_ref, sent_ref):
    slot, core, column = pl.program_id(0), core_ref[0], column_ref[0]
    live = jnp.where(slot < counts_ref[0], 1.0, 0.0)
    kept, sent = cold_ref[0, :, core] * live, cold_ref[0, :, 1 - core] * live
    for parity in range(kept_ref.shape[0]):
        kept_ref[parity, 0] = coef_ref[parity, column] * kept
        sent_ref[parity, 0] = coef_ref[parity, column] * sent


def coded(cold_table, block_ids, counts, group_map, coef, core, ready):
    parities, slots = coef.shape[0], block_ids.shape[0]
    rest = cold_table.shape[1:]
    shape = (parities, slots, rest[0]) + rest[2:]
    out = pl.BlockSpec((parities, 1) + shape[2:], lambda s, *refs: (0, s, 0, 0, 0))
    return pl.pallas_call(
        coded_kernel,
        grid_spec=pltpu.PrefetchScalarGridSpec(
            num_scalar_prefetch=4,
            grid=(slots,),
            in_specs=[
                pl.BlockSpec(memory_space=pltpu.SMEM),
                pl.BlockSpec((1,) + rest, lambda s, ids, *refs: (ids[s], 0, 0, 0, 0)),
                pl.BlockSpec(memory_space=pl.ANY),
            ],
            out_specs=[out, out],
        ),
        out_shape=[jax.ShapeDtypeStruct(shape, jnp.float32)] * 2,
        cost_estimate=pl.CostEstimate(flops=cold_table.size * 3, bytes_accessed=12 * cold_table.size, transcendentals=0),
        compiler_params=pltpu.CompilerParams(vmem_limit_bytes=24 << 20),
        name="coded_blocks",
    )(block_ids, counts, group_map, core.reshape(1), coef, cold_table, ready)


def adagrad_kernel(place_ref, grad_ref, weights_ref, accum_ref, *refs):
    new_weights_ref, new_accum_ref = refs[-2:]
    for block in range(8):
        rows = slice(block * 128, (block + 1) * 128)
        grad = grad_ref[rows, :]
        mean = jnp.mean(grad * grad, axis=1, keepdims=True)
        accum = jnp.transpose(jnp.broadcast_to(accum_ref[block : block + 1, :], (128, 128)))
        new_accum = accum + mean
        new_weights_ref[rows, :] = weights_ref[rows, :] - 0.5 * grad / (jnp.sqrt(new_accum) + 1e-06)
        new_accum_ref[block : block + 1, :] = jnp.transpose(new_accum)[:1, :]


def adagrad_half(place, grad, weights, accum, before=None):
    half, width = grad.shape
    at = lambda i, place: (place[0], 0)
    given = () if before is None else tuple(before)
    return pl.pallas_call(
        adagrad_kernel,
        grid_spec=pltpu.PrefetchScalarGridSpec(
            num_scalar_prefetch=1,
            grid=(1,),
            in_specs=[
                pl.BlockSpec((half, width), lambda i, place: (0, 0)),
                pl.BlockSpec((half, width), at),
                pl.BlockSpec((half // width, width), at),
            ]
            + [pl.BlockSpec(memory_space=pl.ANY)] * len(given),
            out_specs=[pl.BlockSpec((half, width), at), pl.BlockSpec((half // width, width), at)],
        ),
        out_shape=[jax.ShapeDtypeStruct(weights.shape, jnp.float32), jax.ShapeDtypeStruct(accum.shape, jnp.float32)],
        input_output_aliases={4: 0, 5: 1} if given else {},
        cost_estimate=pl.CostEstimate(flops=8 * half * width, bytes_accessed=12 * half * width, transcendentals=half * width),
        compiler_params=pltpu.CompilerParams(vmem_limit_bytes=24 << 20),
        name="hot_rows_adagrad",
    )(place.reshape(1), grad, weights, accum, *given)


def shards(cold_table, block_ids, counts, group_map, coef, batch_ids, out_grad, hot_weights, accum):
    slot_count = block_ids.shape[2]
    block_rows = cold_table.shape[3]
    width = cold_table.shape[4]
    hot_rows = hot_weights.shape[0]
    part_rows = block_rows // 8
    core = lax.axis_index("core")

    half = hot_rows // 2
    theirs = partial_grad(batch_ids[0, 0], out_grad[0, 0], (1 - core) * half, half)
    arrived = swap(theirs, "core")

    table = cold_table[0, 0].reshape(-1, 4, 2, part_rows, width)
    parity, away = coded(table, block_ids[0, 0], counts[0], group_map, coef, core, theirs)
    parity = parity + swap(away, "core")
    parity = parity.reshape(2, slot_count, 2, 2, part_rows, width)
    near_y, far_y = lax.axis_index("yl"), lax.axis_index("ym")
    send_near = pick(parity, 1 - near_y, 3)
    parity = pick(parity, near_y, 3) + swap(send_near, "yl")
    send_far = pick(parity, 1 - far_y, 2)
    parity_shards = (pick(parity, far_y, 2) + swap(send_far, "ym"))[None, None]

    grad = partial_grad(batch_ids[0, 0], out_grad[0, 0], core * half, half) + arrived
    near = size(NEAR)
    parts = exchange(grad.reshape(near, half // near, width), NEAR)
    parts = exchange(sum_copies(parts, size(FAR), send_near), FAR)
    grad = exchange(sum_copies(parts, near, send_far), NEAR).reshape(half, width)
    grad, parity_shards = lax.optimization_barrier((grad, parity_shards))
    other = swap(grad, "core")
    sums = accum.reshape(hot_rows // width, width)
    done = adagrad_half(core, grad, hot_weights, sums)
    new_weights, new_accum = adagrad_half(1 - core, other, hot_weights, sums, done)
    new_accum = new_accum.reshape(hot_rows)
    return (parity_shards, new_weights, new_accum)


def solution(mesh):
    mesh = Mesh(mesh.devices.reshape(SIZES), NAMES)
    in_specs = (
        P(CODE, DP, None, None, None),
        P(CODE, DP, None),
        P(CODE, DP),
        P(CODE),
        P(),
        P(CODE, DP, None),
        P(CODE, DP, None, None),
        P(),
        P(),
    )
    out_specs = (P(CODE, DP, None, None, None, None), P(), P())
    return jax.shard_map(shards, mesh=mesh, in_specs=in_specs, out_specs=out_specs, check_vma=False)
```

```python
import jax
import jax.numpy as jnp
from jax import lax
from jax.experimental import pallas as pl
from jax.experimental.pallas import tpu as pltpu
from jax.sharding import Mesh, PartitionSpec as P

NAMES = ("xh", "xm", "yh", "ym", "yl", "core", "xl", "z")
SIZES = (2, 2, 2, 2, 2, 2, 2, 8)
CODE = ("xh", "xm", "yh", "ym", "yl", "core")
DP = ("xl", "z")
NEAR = ("xh", "xm", "z")
TILE = 256
FAR = ("yh", "ym", "yl", "xl")


def size(axes):
    return lax.axis_size(axes)


def exchange(parts, axes):
    return lax.all_to_all(parts, axes, 0, 0, tiled=True)


def sum_copies_kernel(parts_ref, ready_ref, copies_ref):
    total = parts_ref[0]
    for part in range(1, parts_ref.shape[0]):
        total = total + parts_ref[part]
    copies_ref[...] = jnp.broadcast_to(total[None], copies_ref.shape)


def sum_copies(parts, copies, ready):
    shape = (copies,) + parts.shape[1:]
    return pl.pallas_call(
        sum_copies_kernel,
        out_shape=jax.ShapeDtypeStruct(shape, jnp.float32),
        in_specs=[pl.BlockSpec(memory_space=pltpu.VMEM), pl.BlockSpec(memory_space=pl.ANY)],
        out_specs=pl.BlockSpec(memory_space=pltpu.VMEM),
        cost_estimate=pl.CostEstimate(flops=parts.size, bytes_accessed=4 * parts.size, transcendentals=0),
        compiler_params=pltpu.CompilerParams(vmem_limit_bytes=24 << 20),
        name="sum_copies",
    )(parts, ready)


def swap(value, axis):
    return lax.ppermute(value, axis, [(0, 1), (1, 0)])


def pick(value, place, axis):
    return lax.dynamic_index_in_dim(value, place, axis, keepdims=False)


def sum_kernel(first_ref, ids_ref, rows_ref, *refs):
    arrived, (out_ref, token_ref) = refs[:-2], refs[-2:]
    width = rows_ref.shape[1]
    value = rows_ref[...]
    high = value.astype(jnp.bfloat16)
    rest = value - high.astype(jnp.float32)
    middle = rest.astype(jnp.bfloat16)
    low = (rest - middle.astype(jnp.float32)).astype(jnp.bfloat16)
    three = jnp.concatenate([high, middle, low], axis=1)
    ids = ids_ref[...] - first_ref[0]
    for tile in range(out_ref.shape[0] // TILE):
        row = lax.broadcasted_iota(jnp.int32, (TILE, ids.shape[1]), 0) + tile * TILE
        hit = jnp.where(row == ids, 1.0, 0.0).astype(jnp.bfloat16)
        part = jnp.dot(hit, three, preferred_element_type=jnp.float32)
        total = part[:, :width] + part[:, width : 2 * width] + part[:, 2 * width :]
        here = slice(tile * TILE, (tile + 1) * TILE)
        out_ref[here, :] = total + arrived[0][here, :] if arrived else total
    token_ref[...] = value[:8]


def partial_grad(ids, rows_grad, first, rows, *arrived):
    lookups, width = rows_grad.shape
    whole = pl.BlockSpec(memory_space=pltpu.VMEM)
    return pl.pallas_call(
        sum_kernel,
        out_shape=[jax.ShapeDtypeStruct((rows, width), jnp.float32), jax.ShapeDtypeStruct((8, width), jnp.float32)],
        in_specs=[pl.BlockSpec(memory_space=pltpu.SMEM), whole, whole] + [whole] * len(arrived),
        out_specs=[whole, whole],
        cost_estimate=pl.CostEstimate(flops=6 * rows * lookups * width, bytes_accessed=4 * (lookups + rows) * width, transcendentals=0),
        compiler_params=pltpu.CompilerParams(vmem_limit_bytes=(24 if arrived else 56) << 20),
        name="hot_rows_sum",
    )(first.reshape(1), ids.reshape(1, lookups), rows_grad, *arrived)


def coded_kernel(ids_ref, counts_ref, column_ref, core_ref, coef_ref, cold_ref, ready_ref, kept_ref, sent_ref):
    slot, core, column = pl.program_id(0), core_ref[0], column_ref[0]
    live = jnp.where(slot < counts_ref[0], 1.0, 0.0)
    kept, sent = cold_ref[0, :, core] * live, cold_ref[0, :, 1 - core] * live
    for parity in range(kept_ref.shape[0]):
        kept_ref[parity, 0] = coef_ref[parity, column] * kept
        sent_ref[parity, 0] = coef_ref[parity, column] * sent


def coded(cold_table, block_ids, counts, group_map, coef, core, ready):
    parities, slots = coef.shape[0], block_ids.shape[0]
    rest = cold_table.shape[1:]
    shape = (parities, slots, rest[0]) + rest[2:]
    out = pl.BlockSpec((parities, 1) + shape[2:], lambda s, *refs: (0, s, 0, 0, 0))
    return pl.pallas_call(
        coded_kernel,
        grid_spec=pltpu.PrefetchScalarGridSpec(
            num_scalar_prefetch=4,
            grid=(slots,),
            in_specs=[
                pl.BlockSpec(memory_space=pltpu.SMEM),
                pl.BlockSpec((1,) + rest, lambda s, ids, *refs: (ids[s], 0, 0, 0, 0)),
                pl.BlockSpec(memory_space=pl.ANY),
            ],
            out_specs=[out, out],
        ),
        out_shape=[jax.ShapeDtypeStruct(shape, jnp.float32)] * 2,
        cost_estimate=pl.CostEstimate(flops=cold_table.size * 3, bytes_accessed=12 * cold_table.size, transcendentals=0),
        compiler_params=pltpu.CompilerParams(vmem_limit_bytes=24 << 20),
        name="coded_blocks",
    )(block_ids, counts, group_map, core.reshape(1), coef, cold_table, ready)


def adagrad_kernel(place_ref, grad_ref, weights_ref, accum_ref, *refs):
    new_weights_ref, new_accum_ref = refs[-2:]
    for block in range(8):
        rows = slice(block * 128, (block + 1) * 128)
        grad = grad_ref[rows, :]
        mean = jnp.mean(grad * grad, axis=1, keepdims=True)
        accum = jnp.transpose(jnp.broadcast_to(accum_ref[block : block + 1, :], (128, 128)))
        new_accum = accum + mean
        new_weights_ref[rows, :] = weights_ref[rows, :] - 0.5 * grad / (jnp.sqrt(new_accum) + 1e-06)
        new_accum_ref[block : block + 1, :] = jnp.transpose(new_accum)[:1, :]


def adagrad_half(place, grad, weights, accum, before=None):
    half, width = grad.shape
    at = lambda i, place: (place[0], 0)
    given = () if before is None else tuple(before)
    return pl.pallas_call(
        adagrad_kernel,
        grid_spec=pltpu.PrefetchScalarGridSpec(
            num_scalar_prefetch=1,
            grid=(1,),
            in_specs=[
                pl.BlockSpec((half, width), lambda i, place: (0, 0)),
                pl.BlockSpec((half, width), at),
                pl.BlockSpec((half // width, width), at),
            ]
            + [pl.BlockSpec(memory_space=pl.ANY)] * len(given),
            out_specs=[pl.BlockSpec((half, width), at), pl.BlockSpec((half // width, width), at)],
        ),
        out_shape=[jax.ShapeDtypeStruct(weights.shape, jnp.float32), jax.ShapeDtypeStruct(accum.shape, jnp.float32)],
        input_output_aliases={4: 0, 5: 1} if given else {},
        cost_estimate=pl.CostEstimate(flops=8 * half * width, bytes_accessed=12 * half * width, transcendentals=half * width),
        compiler_params=pltpu.CompilerParams(vmem_limit_bytes=24 << 20),
        name="hot_rows_adagrad",
    )(place.reshape(1), grad, weights, accum, *given)


def shards(cold_table, block_ids, counts, group_map, coef, batch_ids, out_grad, hot_weights, accum):
    slot_count = block_ids.shape[2]
    block_rows = cold_table.shape[3]
    width = cold_table.shape[4]
    hot_rows = hot_weights.shape[0]
    part_rows = block_rows // 8
    core = lax.axis_index("core")

    half = hot_rows // 2
    theirs, token = partial_grad(batch_ids[0, 0], out_grad[0, 0], (1 - core) * half, half)
    arrived = swap(theirs, "core")

    grad, _ = partial_grad(batch_ids[0, 0], out_grad[0, 0], core * half, half, arrived)

    table = cold_table[0, 0].reshape(-1, 4, 2, part_rows, width)
    parity, away = coded(table, block_ids[0, 0], counts[0], group_map, coef, core, token)
    parity = parity + swap(away, "core")
    parity = parity.reshape(2, slot_count, 2, 2, part_rows, width)
    near_y, far_y = lax.axis_index("yl"), lax.axis_index("ym")
    send_near = pick(parity, 1 - near_y, 3)
    parity = pick(parity, near_y, 3) + swap(send_near, "yl")
    send_far = pick(parity, 1 - far_y, 2)
    parity_shards = (pick(parity, far_y, 2) + swap(send_far, "ym"))[None, None]

    near = size(NEAR)
    parts = exchange(grad.reshape(near, half // near, width), NEAR)
    parts = exchange(sum_copies(parts, size(FAR), send_near), FAR)
    grad = exchange(sum_copies(parts, near, send_far), NEAR).reshape(half, width)
    grad, parity_shards = lax.optimization_barrier((grad, parity_shards))
    other = swap(grad, "core")
    sums = accum.reshape(hot_rows // width, width)
    done = adagrad_half(core, grad, hot_weights, sums)
    new_weights, new_accum = adagrad_half(1 - core, other, hot_weights, sums, done)
    new_accum = new_accum.reshape(hot_rows)
    return (parity_shards, new_weights, new_accum)


def solution(mesh):
    mesh = Mesh(mesh.devices.reshape(SIZES), NAMES)
    in_specs = (
        P(CODE, DP, None, None, None),
        P(CODE, DP, None),
        P(CODE, DP),
        P(CODE),
        P(),
        P(CODE, DP, None),
        P(CODE, DP, None, None),
        P(),
        P(),
    )
    out_specs = (P(CODE, DP, None, None, None, None), P(), P())
    return jax.shard_map(shards, mesh=mesh, in_specs=in_specs, out_specs=out_specs, check_vma=False)
```

```python
import jax
import jax.numpy as jnp
from jax import lax
from jax.experimental import pallas as pl
from jax.experimental.pallas import tpu as pltpu
from jax.sharding import Mesh, PartitionSpec as P

NAMES = ("xh", "xm", "yh", "ym", "yl", "core", "xl", "z")
SIZES = (2, 2, 2, 2, 2, 2, 2, 8)
CODE = ("xh", "xm", "yh", "ym", "yl", "core")
DP = ("xl", "z")
NEAR = ("yl", "xl", "z")
TILE = 256
FAR = ("xh", "xm", "yh", "ym")


def size(axes):
    return lax.axis_size(axes)


def exchange(parts, axes):
    return lax.all_to_all(parts, axes, 0, 0, tiled=True)


def sum_copies_kernel(parts_ref, ready_ref, copies_ref):
    total = parts_ref[0]
    for part in range(1, parts_ref.shape[0]):
        total = total + parts_ref[part]
    copies_ref[...] = jnp.broadcast_to(total[None], copies_ref.shape)


def sum_copies(parts, copies, ready):
    shape = (copies,) + parts.shape[1:]
    return pl.pallas_call(
        sum_copies_kernel,
        out_shape=jax.ShapeDtypeStruct(shape, jnp.float32),
        in_specs=[pl.BlockSpec(memory_space=pltpu.VMEM), pl.BlockSpec(memory_space=pl.ANY)],
        out_specs=pl.BlockSpec(memory_space=pltpu.VMEM),
        cost_estimate=pl.CostEstimate(flops=parts.size, bytes_accessed=4 * parts.size, transcendentals=0),
        compiler_params=pltpu.CompilerParams(vmem_limit_bytes=24 << 20),
        name="sum_copies",
    )(parts, ready)


def swap(value, axis):
    return lax.ppermute(value, axis, [(0, 1), (1, 0)])


def pick(value, place, axis):
    return lax.dynamic_index_in_dim(value, place, axis, keepdims=False)


def sum_kernel(first_ref, ids_ref, rows_ref, *refs):
    arrived, out_ref = refs[:-1], refs[-1]
    width = rows_ref.shape[1]
    value = rows_ref[...]
    high = value.astype(jnp.bfloat16)
    rest = value - high.astype(jnp.float32)
    middle = rest.astype(jnp.bfloat16)
    low = (rest - middle.astype(jnp.float32)).astype(jnp.bfloat16)
    three = jnp.concatenate([high, middle, low], axis=1)
    ids = ids_ref[...] - first_ref[0]
    for tile in range(out_ref.shape[0] // TILE):
        row = lax.broadcasted_iota(jnp.int32, (TILE, ids.shape[1]), 0) + tile * TILE
        hit = jnp.where(row == ids, 1.0, 0.0).astype(jnp.bfloat16)
        part = jnp.dot(hit, three, preferred_element_type=jnp.float32)
        total = part[:, :width] + part[:, width : 2 * width] + part[:, 2 * width :]
        here = slice(tile * TILE, (tile + 1) * TILE)
        out_ref[here, :] = total + arrived[0][here, :] if arrived else total


def partial_grad(ids, rows_grad, first, rows, *arrived):
    lookups, width = rows_grad.shape
    whole = pl.BlockSpec(memory_space=pltpu.VMEM)
    return pl.pallas_call(
        sum_kernel,
        out_shape=jax.ShapeDtypeStruct((rows, width), jnp.float32),
        in_specs=[pl.BlockSpec(memory_space=pltpu.SMEM), whole, whole] + [whole] * len(arrived),
        out_specs=whole,
        cost_estimate=pl.CostEstimate(flops=6 * rows * lookups * width, bytes_accessed=4 * (lookups + rows) * width, transcendentals=0),
        compiler_params=pltpu.CompilerParams(vmem_limit_bytes=(24 if arrived else 56) << 20),
        name="hot_rows_sum",
    )(first.reshape(1), ids.reshape(1, lookups), rows_grad, *arrived)


def coded_kernel(ids_ref, counts_ref, column_ref, core_ref, coef_ref, cold_ref, kept_ref, sent_ref):
    slot, core, column = pl.program_id(0), core_ref[0], column_ref[0]
    live = jnp.where(slot < counts_ref[0, 0], 1.0, 0.0)
    kept, sent = cold_ref[0, :, core] * live, cold_ref[0, :, 1 - core] * live
    for parity in range(kept_ref.shape[0]):
        kept_ref[parity, 0] = coef_ref[parity, column] * kept
        sent_ref[parity, 0] = coef_ref[parity, column] * sent


def coded(cold_table, block_ids, counts, group_map, coef, core):
    parities, slots = coef.shape[0], block_ids.shape[2]
    rest = cold_table.shape[1:]
    shape = (parities, slots, rest[0]) + rest[2:]
    out = pl.BlockSpec((parities, 1) + shape[2:], lambda s, *refs: (0, s, 0, 0, 0))
    return pl.pallas_call(
        coded_kernel,
        grid_spec=pltpu.PrefetchScalarGridSpec(
            num_scalar_prefetch=4,
            grid=(slots,),
            in_specs=[
                pl.BlockSpec(memory_space=pltpu.SMEM),
                pl.BlockSpec((1,) + rest, lambda s, ids, *refs: (ids[0, 0, s], 0, 0, 0, 0)),
            ],
            out_specs=[out, out],
        ),
        out_shape=[jax.ShapeDtypeStruct(shape, jnp.float32)] * 2,
        cost_estimate=pl.CostEstimate(flops=cold_table.size * 3, bytes_accessed=12 * cold_table.size, transcendentals=0),
        compiler_params=pltpu.CompilerParams(vmem_limit_bytes=24 << 20),
        name="coded_blocks",
    )(block_ids, counts, group_map, core.reshape(1), coef, cold_table)


def adagrad_kernel(place_ref, grad_ref, weights_ref, accum_ref, *refs):
    new_weights_ref, new_accum_ref = refs[-2:]
    for block in range(8):
        rows = slice(block * 128, (block + 1) * 128)
        grad = grad_ref[rows, :]
        mean = jnp.mean(grad * grad, axis=1, keepdims=True)
        accum = jnp.transpose(jnp.broadcast_to(accum_ref[block : block + 1, :], (128, 128)))
        new_accum = accum + mean
        new_weights_ref[rows, :] = weights_ref[rows, :] - 0.5 * grad / (jnp.sqrt(new_accum) + 1e-06)
        new_accum_ref[block : block + 1, :] = jnp.transpose(new_accum)[:1, :]


def adagrad_half(place, grad, weights, accum, before=None):
    half, width = grad.shape
    at = lambda i, place: (place[0], 0)
    given = () if before is None else tuple(before)
    return pl.pallas_call(
        adagrad_kernel,
        grid_spec=pltpu.PrefetchScalarGridSpec(
            num_scalar_prefetch=1,
            grid=(1,),
            in_specs=[
                pl.BlockSpec((half, width), lambda i, place: (0, 0)),
                pl.BlockSpec((half, width), at),
                pl.BlockSpec((half // width, width), at),
            ]
            + [pl.BlockSpec(memory_space=pl.ANY)] * len(given),
            out_specs=[pl.BlockSpec((half, width), at), pl.BlockSpec((half // width, width), at)],
        ),
        out_shape=[jax.ShapeDtypeStruct(weights.shape, jnp.float32), jax.ShapeDtypeStruct(accum.shape, jnp.float32)],
        input_output_aliases={4: 0, 5: 1} if given else {},
        cost_estimate=pl.CostEstimate(flops=8 * half * width, bytes_accessed=12 * half * width, transcendentals=half * width),
        compiler_params=pltpu.CompilerParams(vmem_limit_bytes=24 << 20),
        name="hot_rows_adagrad",
    )(place.reshape(1), grad, weights, accum, *given)


def shards(cold_table, block_ids, counts, group_map, coef, batch_ids, out_grad, hot_weights, accum):
    slot_count = block_ids.shape[2]
    block_rows = cold_table.shape[3]
    width = cold_table.shape[4]
    hot_rows = hot_weights.shape[0]
    part_rows = block_rows // 8
    core = lax.axis_index("core")

    half = hot_rows // 2
    theirs = partial_grad(batch_ids[0, 0], out_grad[0, 0], (1 - core) * half, half)
    arrived = swap(theirs, "core")

    grad = partial_grad(batch_ids[0, 0], out_grad[0, 0], core * half, half, arrived)

    cold_table, theirs = lax.optimization_barrier((cold_table, theirs))
    table = cold_table[0, 0].reshape(-1, 4, 2, part_rows, width)
    parity, away = coded(table, block_ids, counts, group_map, coef, core)
    parity = parity + swap(away, "core")
    parity = parity.reshape(2, slot_count, 2, 2, part_rows, width)
    near_y, far_y = lax.axis_index("yl"), lax.axis_index("ym")
    send_near = pick(parity, 1 - near_y, 3)
    parity = pick(parity, near_y, 3) + swap(send_near, "yl")
    send_far = pick(parity, 1 - far_y, 2)
    parity_shards = (pick(parity, far_y, 2) + swap(send_far, "ym"))[None, None]

    near = size(NEAR)
    parts = exchange(grad.reshape(near, half // near, width), NEAR)
    parts = exchange(sum_copies(parts, size(FAR), send_near), FAR)
    grad = exchange(sum_copies(parts, near, send_far), NEAR).reshape(half, width)
    grad, parity_shards = lax.optimization_barrier((grad, parity_shards))
    other = swap(grad, "core")
    sums = accum.reshape(hot_rows // width, width)
    done = adagrad_half(core, grad, hot_weights, sums)
    new_weights, new_accum = adagrad_half(1 - core, other, hot_weights, sums, done)
    new_accum = new_accum.reshape(hot_rows)
    return (parity_shards, new_weights, new_accum)


def solution(mesh):
    mesh = Mesh(mesh.devices.reshape(SIZES), NAMES)
    in_specs = (
        P(CODE, DP, None, None, None),
        P(CODE, DP, None),
        P(CODE, DP),
        P(CODE),
        P(),
        P(CODE, DP, None),
        P(CODE, DP, None, None),
        P(),
        P(),
    )
    out_specs = (P(CODE, DP, None, None, None, None), P(), P())
    return jax.shard_map(shards, mesh=mesh, in_specs=in_specs, out_specs=out_specs, check_vma=False)
```

```python
import jax
import jax.numpy as jnp
from jax import lax
from jax.experimental import pallas as pl
from jax.experimental.pallas import tpu as pltpu
from jax.sharding import Mesh, PartitionSpec as P

NAMES = ("xh", "xm", "yh", "ym", "yl", "core", "xl", "z")
SIZES = (2, 2, 2, 2, 2, 2, 2, 8)
CODE = ("xh", "xm", "yh", "ym", "yl", "core")
DP = ("xl", "z")
NEAR = ("yl", "xl", "z")
TILE = 256
FAR = ("xh", "xm", "yh", "ym")


def size(axes):
    return lax.axis_size(axes)


def exchange(parts, axes):
    return lax.all_to_all(parts, axes, 0, 0, tiled=True)


def sum_copies_kernel(parts_ref, ready_ref, copies_ref):
    total = parts_ref[0]
    for part in range(1, parts_ref.shape[0]):
        total = total + parts_ref[part]
    copies_ref[...] = jnp.broadcast_to(total[None], copies_ref.shape)


def sum_copies(parts, copies, ready):
    shape = (copies,) + parts.shape[1:]
    return pl.pallas_call(
        sum_copies_kernel,
        out_shape=jax.ShapeDtypeStruct(shape, jnp.float32),
        in_specs=[pl.BlockSpec(memory_space=pltpu.VMEM), pl.BlockSpec(memory_space=pl.ANY)],
        out_specs=pl.BlockSpec(memory_space=pltpu.VMEM),
        cost_estimate=pl.CostEstimate(flops=parts.size, bytes_accessed=4 * parts.size, transcendentals=0),
        compiler_params=pltpu.CompilerParams(vmem_limit_bytes=24 << 20),
        name="sum_copies",
    )(parts, ready)


def swap(value, axis):
    return lax.ppermute(value, axis, [(0, 1), (1, 0)])


def pick(value, place, axis):
    return lax.dynamic_index_in_dim(value, place, axis, keepdims=False)


def three_parts(value):
    high = value.astype(jnp.bfloat16)
    rest = value - high.astype(jnp.float32)
    middle = rest.astype(jnp.bfloat16)
    low = (rest - middle.astype(jnp.float32)).astype(jnp.bfloat16)
    return jnp.concatenate([high, middle, low], axis=1)


def tile_sum(ids, three, tile):
    row = lax.broadcasted_iota(jnp.int32, (TILE, ids.shape[1]), 0) + tile * TILE
    hit = jnp.where(row == ids, 1.0, 0.0).astype(jnp.bfloat16)
    part = jnp.dot(hit, three, preferred_element_type=jnp.float32)
    width = three.shape[1] // 3
    return part[:, :width] + part[:, width : 2 * width] + part[:, 2 * width :]


def sum_kernel(core_ref, ids_ref, rows_ref, arrived_ref, out_ref):
    three = three_parts(rows_ref[...])
    ids = ids_ref[...] - core_ref[0] * out_ref.shape[0]
    for tile in range(out_ref.shape[0] // TILE):
        here = slice(tile * TILE, (tile + 1) * TILE)
        out_ref[here, :] = tile_sum(ids, three, tile) + arrived_ref[here, :]


def own_half(core, ids, rows_grad, arrived):
    lookups, width = rows_grad.shape
    rows = arrived.shape[0]
    whole = pl.BlockSpec(memory_space=pltpu.VMEM)
    return pl.pallas_call(
        sum_kernel,
        out_shape=jax.ShapeDtypeStruct((rows, width), jnp.float32),
        in_specs=[pl.BlockSpec(memory_space=pltpu.SMEM), whole, whole, whole],
        out_specs=whole,
        cost_estimate=pl.CostEstimate(flops=6 * rows * lookups * width, bytes_accessed=4 * (lookups + 2 * rows) * width, transcendentals=0),
        compiler_params=pltpu.CompilerParams(vmem_limit_bytes=24 << 20),
        name="hot_rows_sum",
    )(core.reshape(1), ids, rows_grad, arrived)


def front_kernel(core_ref, blocks_ref, counts_ref, column_ref, coef_ref, ids_ref, rows_ref, cold_ref, *refs):
    outs, (blocks, *made, came, left) = refs[:3], refs[3:]
    theirs, kept, sent = made
    slots, half = blocks.shape[0], theirs.shape[0]
    core, column = core_ref[0], column_ref[0]
    loads = [pltpu.make_async_copy(cold_ref.at[blocks_ref[0, 0, s]], blocks.at[s], came.at[s]) for s in range(slots)]
    for load in loads:
        load.start()
    three = three_parts(rows_ref[...])
    ids = ids_ref[...] - (1 - core) * half
    for tile in range(half // TILE):
        theirs[tile * TILE : (tile + 1) * TILE, :] = tile_sum(ids, three, tile)
    stores = [pltpu.make_async_copy(theirs, outs[0], left.at[0])]
    stores[0].start()
    for s in range(slots):
        loads[s].wait()
        live = jnp.where(s < counts_ref[0, 0], 1.0, 0.0)
        for parity in range(kept.shape[0]):
            scale = coef_ref[parity, column] * live
            kept[parity, s] = scale * blocks[s, :, core]
            sent[parity, s] = scale * blocks[s, :, 1 - core]
        for place, (made_here, out) in enumerate(((kept, outs[1]), (sent, outs[2]))):
            store = pltpu.make_async_copy(made_here.at[:, s], out.at[:, s], left.at[1 + 2 * s + place])
            store.start()
            stores.append(store)
    for store in stores:
        store.wait()


def front(core, block_ids, counts, group_map, coef, ids, rows_grad, cold_table, half):
    slots, parities, width = block_ids.shape[2], coef.shape[0], rows_grad.shape[1]
    rest = cold_table.shape[1:]
    coded = jax.ShapeDtypeStruct((parities, slots, rest[0]) + rest[2:], jnp.float32)
    outs = [jax.ShapeDtypeStruct((half, width), jnp.float32), coded, coded]
    scalar, whole, apart = (pl.BlockSpec(memory_space=space) for space in (pltpu.SMEM, pltpu.VMEM, pl.ANY))
    return pl.pallas_call(
        front_kernel,
        out_shape=outs,
        in_specs=[scalar] * 5 + [whole] * 2 + [apart],
        out_specs=[apart] * 3,
        scratch_shapes=[pltpu.VMEM((slots,) + rest, jnp.float32)]
        + [pltpu.VMEM(out.shape, out.dtype) for out in outs]
        + [pltpu.SemaphoreType.DMA((slots,)), pltpu.SemaphoreType.DMA((1 + 2 * slots,))],
        cost_estimate=pl.CostEstimate(flops=6 * half * rows_grad.size, bytes_accessed=4 << 20, transcendentals=0),
        compiler_params=pltpu.CompilerParams(vmem_limit_bytes=56 << 20),
        name="front",
    )(core.reshape(1), block_ids, counts, group_map, coef, ids, rows_grad, cold_table)


def adagrad_kernel(place_ref, grad_ref, weights_ref, accum_ref, *refs):
    new_weights_ref, new_accum_ref = refs[-2:]
    for block in range(8):
        rows = slice(block * 128, (block + 1) * 128)
        grad = grad_ref[rows, :]
        mean = jnp.mean(grad * grad, axis=1, keepdims=True)
        accum = jnp.transpose(jnp.broadcast_to(accum_ref[block : block + 1, :], (128, 128)))
        new_accum = accum + mean
        new_weights_ref[rows, :] = weights_ref[rows, :] - 0.5 * grad / (jnp.sqrt(new_accum) + 1e-06)
        new_accum_ref[block : block + 1, :] = jnp.transpose(new_accum)[:1, :]


def adagrad_half(place, grad, weights, accum, before=None):
    half, width = grad.shape
    at = lambda i, place: (place[0], 0)
    given = () if before is None else tuple(before)
    return pl.pallas_call(
        adagrad_kernel,
        grid_spec=pltpu.PrefetchScalarGridSpec(
            num_scalar_prefetch=1,
            grid=(1,),
            in_specs=[
                pl.BlockSpec((half, width), lambda i, place: (0, 0)),
                pl.BlockSpec((half, width), at),
                pl.BlockSpec((half // width, width), at),
            ]
            + [pl.BlockSpec(memory_space=pl.ANY)] * len(given),
            out_specs=[pl.BlockSpec((half, width), at), pl.BlockSpec((half // width, width), at)],
        ),
        out_shape=[jax.ShapeDtypeStruct(weights.shape, jnp.float32), jax.ShapeDtypeStruct(accum.shape, jnp.float32)],
        input_output_aliases={4: 0, 5: 1} if given else {},
        cost_estimate=pl.CostEstimate(flops=8 * half * width, bytes_accessed=12 * half * width, transcendentals=half * width),
        compiler_params=pltpu.CompilerParams(vmem_limit_bytes=24 << 20),
        name="hot_rows_adagrad",
    )(place.reshape(1), grad, weights, accum, *given)


def shards(cold_table, block_ids, counts, group_map, coef, batch_ids, out_grad, hot_weights, accum):
    slot_count = block_ids.shape[2]
    block_rows = cold_table.shape[3]
    width = cold_table.shape[4]
    hot_rows = hot_weights.shape[0]
    part_rows = block_rows // 8
    core = lax.axis_index("core")

    half = hot_rows // 2
    ids, rows_grad = batch_ids[0], out_grad[0, 0]
    table = cold_table[0, 0].reshape(-1, 4, 2, part_rows, width)
    theirs, parity, away = front(core, block_ids, counts, group_map, coef, ids, rows_grad, table, half)
    arrived = swap(theirs, "core")
    grad = own_half(core, ids, rows_grad, arrived)
    parity = parity + swap(away, "core")
    parity = parity.reshape(2, slot_count, 2, 2, part_rows, width)
    near_y, far_y = lax.axis_index("yl"), lax.axis_index("ym")
    send_near = pick(parity, 1 - near_y, 3)
    parity = pick(parity, near_y, 3) + swap(send_near, "yl")
    send_far = pick(parity, 1 - far_y, 2)
    parity_shards = (pick(parity, far_y, 2) + swap(send_far, "ym"))[None, None]

    near = size(NEAR)
    parts = exchange(grad.reshape(near, half // near, width), NEAR)
    parts = exchange(sum_copies(parts, size(FAR), send_near), FAR)
    grad = exchange(sum_copies(parts, near, send_far), NEAR).reshape(half, width)
    grad, parity_shards = lax.optimization_barrier((grad, parity_shards))
    other = swap(grad, "core")
    sums = accum.reshape(hot_rows // width, width)
    done = adagrad_half(core, grad, hot_weights, sums)
    new_weights, new_accum = adagrad_half(1 - core, other, hot_weights, sums, done)
    new_accum = new_accum.reshape(hot_rows)
    return (parity_shards, new_weights, new_accum)


def solution(mesh):
    mesh = Mesh(mesh.devices.reshape(SIZES), NAMES)
    in_specs = (
        P(CODE, DP, None, None, None),
        P(CODE, DP, None),
        P(CODE, DP),
        P(CODE),
        P(),
        P(CODE, DP, None),
        P(CODE, DP, None, None),
        P(),
        P(),
    )
    out_specs = (P(CODE, DP, None, None, None, None), P(), P())
    return jax.shard_map(shards, mesh=mesh, in_specs=in_specs, out_specs=out_specs, check_vma=False)
```

```python
import jax
import jax.numpy as jnp
from jax import lax
from jax.experimental import pallas as pl
from jax.experimental.pallas import tpu as pltpu
from jax.sharding import Mesh, PartitionSpec as P

NAMES = ("xh", "xm", "yh", "ym", "yl", "core", "xl", "z")
SIZES = (2, 2, 2, 2, 2, 2, 2, 8)
CODE = ("xh", "xm", "yh", "ym", "yl", "core")
DP = ("xl", "z")
NEAR = ("xh", "xm", "xl", "z")
TILE = 256
FAR = ("yh", "ym", "yl")


def size(axes):
    return lax.axis_size(axes)


def exchange(parts, axes):
    return lax.all_to_all(parts, axes, 0, 0, tiled=True)


def sum_copies_kernel(parts_ref, ready_ref, copies_ref):
    total = parts_ref[0]
    for part in range(1, parts_ref.shape[0]):
        total = total + parts_ref[part]
    copies_ref[...] = jnp.broadcast_to(total[None], copies_ref.shape)


def sum_copies(parts, copies, ready):
    shape = (copies,) + parts.shape[1:]
    return pl.pallas_call(
        sum_copies_kernel,
        out_shape=jax.ShapeDtypeStruct(shape, jnp.float32),
        in_specs=[pl.BlockSpec(memory_space=pltpu.VMEM), pl.BlockSpec(memory_space=pl.ANY)],
        out_specs=pl.BlockSpec(memory_space=pltpu.VMEM),
        cost_estimate=pl.CostEstimate(flops=parts.size, bytes_accessed=4 * parts.size, transcendentals=0),
        compiler_params=pltpu.CompilerParams(vmem_limit_bytes=24 << 20),
        name="sum_copies",
    )(parts, ready)


def swap(value, axis):
    return lax.ppermute(value, axis, [(0, 1), (1, 0)])


def pick(value, place, axis):
    return lax.dynamic_index_in_dim(value, place, axis, keepdims=False)


def three_parts(value):
    high = value.astype(jnp.bfloat16)
    rest = value - high.astype(jnp.float32)
    middle = rest.astype(jnp.bfloat16)
    low = (rest - middle.astype(jnp.float32)).astype(jnp.bfloat16)
    return jnp.concatenate([high, middle, low], axis=1)


def tile_sum(ids, three, tile):
    row = lax.broadcasted_iota(jnp.int32, (TILE, ids.shape[1]), 0) + tile * TILE
    hit = jnp.where(row == ids, 1.0, 0.0).astype(jnp.bfloat16)
    part = jnp.dot(hit, three, preferred_element_type=jnp.float32)
    width = three.shape[1] // 3
    return part[:, :width] + part[:, width : 2 * width] + part[:, 2 * width :]


def sum_kernel(core_ref, ids_ref, rows_ref, out_ref):
    three = three_parts(rows_ref[...])
    ids = ids_ref[...] - core_ref[0] * out_ref.shape[0]
    for tile in range(out_ref.shape[0] // TILE):
        here = slice(tile * TILE, (tile + 1) * TILE)
        out_ref[here, :] = tile_sum(ids, three, tile)


def add_kernel(left_ref, right_ref, out_ref):
    out_ref[...] = left_ref[...] + right_ref[...]


def added(left, right):
    return pl.pallas_call(
        add_kernel,
        out_shape=jax.ShapeDtypeStruct(left.shape, left.dtype),
        in_specs=[pl.BlockSpec(memory_space=pltpu.VMEM)] * 2,
        out_specs=pl.BlockSpec(memory_space=pltpu.VMEM),
        compiler_params=pltpu.CompilerParams(vmem_limit_bytes=24 << 20),
        name="added",
    )(left, right)


def own_half(core, ids, rows_grad, rows):
    lookups, width = rows_grad.shape
    whole = pl.BlockSpec(memory_space=pltpu.VMEM)
    return pl.pallas_call(
        sum_kernel,
        out_shape=jax.ShapeDtypeStruct((rows, width), jnp.float32),
        in_specs=[pl.BlockSpec(memory_space=pltpu.SMEM), whole, whole],
        out_specs=whole,
        cost_estimate=pl.CostEstimate(flops=6 * rows * lookups * width, bytes_accessed=4 * (lookups + rows) * width, transcendentals=0),
        compiler_params=pltpu.CompilerParams(vmem_limit_bytes=24 << 20),
        name="hot_rows_sum",
    )(core.reshape(1), ids, rows_grad)


def front_kernel(core_ref, blocks_ref, counts_ref, column_ref, coef_ref, ids_ref, rows_ref, cold_ref, *refs):
    outs, (blocks, *made, came, left) = refs[:3], refs[3:]
    theirs, kept, sent = made
    slots, half = blocks.shape[0], theirs.shape[0]
    core, column = core_ref[0], column_ref[0]
    loads = [pltpu.make_async_copy(cold_ref.at[blocks_ref[0, 0, s]], blocks.at[s], came.at[s]) for s in range(slots)]
    for load in loads:
        load.start()
    three = three_parts(rows_ref[...])
    ids = ids_ref[...] - (1 - core) * half
    for tile in range(half // TILE):
        theirs[tile * TILE : (tile + 1) * TILE, :] = tile_sum(ids, three, tile)
    stores = [pltpu.make_async_copy(theirs, outs[0], left.at[0])]
    stores[0].start()
    for s in range(slots):
        loads[s].wait()
        live = jnp.where(s < counts_ref[0, 0], 1.0, 0.0)
        for parity in range(kept.shape[0]):
            scale = coef_ref[parity, column] * live
            kept[parity, s] = scale * blocks[s, :, core]
            sent[parity, s] = scale * blocks[s, :, 1 - core]
        for place, (made_here, out) in enumerate(((kept, outs[1]), (sent, outs[2]))):
            store = pltpu.make_async_copy(made_here.at[:, s], out.at[:, s], left.at[1 + 2 * s + place])
            store.start()
            stores.append(store)
    for store in stores:
        store.wait()


def front(core, block_ids, counts, group_map, coef, ids, rows_grad, cold_table, half):
    slots, parities, width = block_ids.shape[2], coef.shape[0], rows_grad.shape[1]
    rest = cold_table.shape[1:]
    coded = jax.ShapeDtypeStruct((parities, slots, rest[0]) + rest[2:], jnp.float32)
    outs = [jax.ShapeDtypeStruct((half, width), jnp.float32), coded, coded]
    scalar, whole, apart = (pl.BlockSpec(memory_space=space) for space in (pltpu.SMEM, pltpu.VMEM, pl.ANY))
    return pl.pallas_call(
        front_kernel,
        out_shape=outs,
        in_specs=[scalar] * 5 + [whole] * 2 + [apart],
        out_specs=[apart] * 3,
        scratch_shapes=[pltpu.VMEM((slots,) + rest, jnp.float32)]
        + [pltpu.VMEM(out.shape, out.dtype) for out in outs]
        + [pltpu.SemaphoreType.DMA((slots,)), pltpu.SemaphoreType.DMA((1 + 2 * slots,))],
        cost_estimate=pl.CostEstimate(flops=6 * half * rows_grad.size, bytes_accessed=4 << 20, transcendentals=0),
        compiler_params=pltpu.CompilerParams(vmem_limit_bytes=56 << 20),
        name="front",
    )(core.reshape(1), block_ids, counts, group_map, coef, ids, rows_grad, cold_table)


def adagrad_kernel(place_ref, grad_ref, weights_ref, accum_ref, *refs):
    new_weights_ref, new_accum_ref = refs[-2:]
    for block in range(8):
        rows = slice(block * 128, (block + 1) * 128)
        grad = grad_ref[rows, :]
        mean = jnp.mean(grad * grad, axis=1, keepdims=True)
        accum = jnp.transpose(jnp.broadcast_to(accum_ref[block : block + 1, :], (128, 128)))
        new_accum = accum + mean
        new_weights_ref[rows, :] = weights_ref[rows, :] - 0.5 * grad / (jnp.sqrt(new_accum) + 1e-06)
        new_accum_ref[block : block + 1, :] = jnp.transpose(new_accum)[:1, :]


def adagrad_half(place, grad, weights, accum, before=None):
    half, width = grad.shape
    at = lambda i, place: (place[0], 0)
    given = () if before is None else tuple(before)
    return pl.pallas_call(
        adagrad_kernel,
        grid_spec=pltpu.PrefetchScalarGridSpec(
            num_scalar_prefetch=1,
            grid=(1,),
            in_specs=[
                pl.BlockSpec((half, width), lambda i, place: (0, 0)),
                pl.BlockSpec((half, width), at),
                pl.BlockSpec((half // width, width), at),
            ]
            + [pl.BlockSpec(memory_space=pl.ANY)] * len(given),
            out_specs=[pl.BlockSpec((half, width), at), pl.BlockSpec((half // width, width), at)],
        ),
        out_shape=[jax.ShapeDtypeStruct(weights.shape, jnp.float32), jax.ShapeDtypeStruct(accum.shape, jnp.float32)],
        input_output_aliases={4: 0, 5: 1} if given else {},
        cost_estimate=pl.CostEstimate(flops=8 * half * width, bytes_accessed=12 * half * width, transcendentals=half * width),
        compiler_params=pltpu.CompilerParams(vmem_limit_bytes=24 << 20),
        name="hot_rows_adagrad",
    )(place.reshape(1), grad, weights, accum, *given)


def shards(cold_table, block_ids, counts, group_map, coef, batch_ids, out_grad, hot_weights, accum):
    slot_count = block_ids.shape[2]
    block_rows = cold_table.shape[3]
    width = cold_table.shape[4]
    hot_rows = hot_weights.shape[0]
    part_rows = block_rows // 8
    core = lax.axis_index("core")

    half = hot_rows // 2
    ids, rows_grad = batch_ids[0], out_grad[0, 0]
    table = cold_table[0, 0].reshape(-1, 4, 2, part_rows, width)
    theirs, parity, away = front(core, block_ids, counts, group_map, coef, ids, rows_grad, table, half)
    arrived = swap(theirs, "core")
    grad = added(own_half(core, ids, rows_grad, half), arrived)
    away, grad = lax.optimization_barrier((away, grad))
    parity = parity + swap(away, "core")
    parity = parity.reshape(2, slot_count, 2, 2, part_rows, width)
    near_y, far_y = lax.axis_index("yl"), lax.axis_index("ym")
    send_near = pick(parity, 1 - near_y, 3)
    parity = pick(parity, near_y, 3) + swap(send_near, "yl")
    send_far = pick(parity, 1 - far_y, 2)
    mine, last = pick(parity, far_y, 2), swap(send_far, "ym")

    near = size(NEAR)
    parts = exchange(grad.reshape(near, half // near, width), NEAR)
    parts = exchange(sum_copies(parts, size(FAR), send_near), FAR)
    grad = exchange(sum_copies(parts, near, send_far), NEAR).reshape(half, width)
    grad, last = lax.optimization_barrier((grad, last))
    parity_shards = (mine + last)[None, None]
    other = swap(grad, "core")
    sums = accum.reshape(hot_rows // width, width)
    done = adagrad_half(core, grad, hot_weights, sums)
    new_weights, new_accum = adagrad_half(1 - core, other, hot_weights, sums, done)
    new_accum = new_accum.reshape(hot_rows)
    return (parity_shards, new_weights, new_accum)


def solution(mesh):
    mesh = Mesh(mesh.devices.reshape(SIZES), NAMES)
    in_specs = (
        P(CODE, DP, None, None, None),
        P(CODE, DP, None),
        P(CODE, DP),
        P(CODE),
        P(),
        P(CODE, DP, None),
        P(CODE, DP, None, None),
        P(),
        P(),
    )
    out_specs = (P(CODE, DP, None, None, None, None), P(), P())
    return jax.shard_map(shards, mesh=mesh, in_specs=in_specs, out_specs=out_specs, check_vma=False)
```

```python
import jax
import jax.numpy as jnp
from jax import lax
from jax.experimental import pallas as pl
from jax.experimental.pallas import tpu as pltpu
from jax.sharding import Mesh, PartitionSpec as P

NAMES = ("xh", "xm", "yh", "ym", "yl", "core", "xl", "z")
SIZES = (2, 2, 2, 2, 2, 2, 2, 8)
CODE = ("xh", "xm", "yh", "ym", "yl", "core")
DP = ("xl", "z")
NEAR = ("z", "xh", "xm", "xl")
TILE = 256
FAR = ("yh", "ym", "yl")


def size(axes):
    return lax.axis_size(axes)


def exchange(parts, axes):
    return lax.all_to_all(parts, axes, 0, 0, tiled=True)


def sum_copies_kernel(parts_ref, ready_ref, copies_ref):
    total = parts_ref[0]
    for part in range(1, parts_ref.shape[0]):
        total = total + parts_ref[part]
    copies_ref[...] = jnp.broadcast_to(total[None], copies_ref.shape)


def sum_copies(parts, copies, ready):
    shape = (copies,) + parts.shape[1:]
    return pl.pallas_call(
        sum_copies_kernel,
        out_shape=jax.ShapeDtypeStruct(shape, jnp.float32),
        in_specs=[pl.BlockSpec(memory_space=pltpu.VMEM), pl.BlockSpec(memory_space=pl.ANY)],
        out_specs=pl.BlockSpec(memory_space=pltpu.VMEM),
        cost_estimate=pl.CostEstimate(flops=parts.size, bytes_accessed=4 * parts.size, transcendentals=0),
        compiler_params=pltpu.CompilerParams(vmem_limit_bytes=24 << 20),
        name="sum_copies",
    )(parts, ready)


def swap(value, axis):
    return lax.ppermute(value, axis, [(0, 1), (1, 0)])


def pick(value, place, axis):
    return lax.dynamic_index_in_dim(value, place, axis, keepdims=False)


def three_parts(value):
    high = value.astype(jnp.bfloat16)
    rest = value - high.astype(jnp.float32)
    middle = rest.astype(jnp.bfloat16)
    low = (rest - middle.astype(jnp.float32)).astype(jnp.bfloat16)
    return jnp.concatenate([high, middle, low], axis=1)


def tile_sum(ids, three, tile):
    row = lax.broadcasted_iota(jnp.int32, (TILE, ids.shape[1]), 0) + tile * TILE
    hit = jnp.where(row == ids, 1.0, 0.0).astype(jnp.bfloat16)
    part = jnp.dot(hit, three, preferred_element_type=jnp.float32)
    width = three.shape[1] // 3
    return part[:, :width] + part[:, width : 2 * width] + part[:, 2 * width :]


def sum_kernel(core_ref, ids_ref, rows_ref, out_ref):
    three = three_parts(rows_ref[...])
    ids = ids_ref[...] - core_ref[0] * out_ref.shape[0]
    for tile in range(out_ref.shape[0] // TILE):
        here = slice(tile * TILE, (tile + 1) * TILE)
        out_ref[here, :] = tile_sum(ids, three, tile)


def add_kernel(left_ref, right_ref, out_ref):
    out_ref[...] = left_ref[...] + right_ref[...]


def added(left, right):
    return pl.pallas_call(
        add_kernel,
        out_shape=jax.ShapeDtypeStruct(left.shape, left.dtype),
        in_specs=[pl.BlockSpec(memory_space=pltpu.VMEM)] * 2,
        out_specs=pl.BlockSpec(memory_space=pltpu.VMEM),
        compiler_params=pltpu.CompilerParams(vmem_limit_bytes=24 << 20),
        name="added",
    )(left, right)


def own_half(core, ids, rows_grad, rows):
    lookups, width = rows_grad.shape
    whole = pl.BlockSpec(memory_space=pltpu.VMEM)
    return pl.pallas_call(
        sum_kernel,
        out_shape=jax.ShapeDtypeStruct((rows, width), jnp.float32),
        in_specs=[pl.BlockSpec(memory_space=pltpu.SMEM), whole, whole],
        out_specs=whole,
        cost_estimate=pl.CostEstimate(flops=6 * rows * lookups * width, bytes_accessed=4 * (lookups + rows) * width, transcendentals=0),
        compiler_params=pltpu.CompilerParams(vmem_limit_bytes=24 << 20),
        name="hot_rows_sum",
    )(core.reshape(1), ids, rows_grad)


def front_kernel(core_ref, blocks_ref, counts_ref, column_ref, coef_ref, ids_ref, rows_ref, cold_ref, *refs):
    outs, (blocks, *made, came, left) = refs[:3], refs[3:]
    theirs, kept, sent = made
    slots, half = blocks.shape[0], theirs.shape[0]
    core, column = core_ref[0], column_ref[0]
    loads = [pltpu.make_async_copy(cold_ref.at[blocks_ref[0, 0, s]], blocks.at[s], came.at[s]) for s in range(slots)]
    for load in loads:
        load.start()
    three = three_parts(rows_ref[...])
    ids = ids_ref[...] - (1 - core) * half
    for tile in range(half // TILE):
        theirs[tile * TILE : (tile + 1) * TILE, :] = tile_sum(ids, three, tile)
    stores = [pltpu.make_async_copy(theirs, outs[0], left.at[0])]
    stores[0].start()
    for s in range(slots):
        loads[s].wait()
        live = jnp.where(s < counts_ref[0, 0], 1.0, 0.0)
        for parity in range(kept.shape[0]):
            scale = coef_ref[parity, column] * live
            kept[parity, s] = scale * blocks[s, :, core]
            sent[parity, s] = scale * blocks[s, :, 1 - core]
        for place, (made_here, out) in enumerate(((kept, outs[1]), (sent, outs[2]))):
            store = pltpu.make_async_copy(made_here.at[:, s], out.at[:, s], left.at[1 + 2 * s + place])
            store.start()
            stores.append(store)
    for store in stores:
        store.wait()


def front(core, block_ids, counts, group_map, coef, ids, rows_grad, cold_table, half):
    slots, parities, width = block_ids.shape[2], coef.shape[0], rows_grad.shape[1]
    rest = cold_table.shape[1:]
    coded = jax.ShapeDtypeStruct((parities, slots, rest[0]) + rest[2:], jnp.float32)
    outs = [jax.ShapeDtypeStruct((half, width), jnp.float32), coded, coded]
    scalar, whole, apart = (pl.BlockSpec(memory_space=space) for space in (pltpu.SMEM, pltpu.VMEM, pl.ANY))
    return pl.pallas_call(
        front_kernel,
        out_shape=outs,
        in_specs=[scalar] * 5 + [whole] * 2 + [apart],
        out_specs=[apart] * 3,
        scratch_shapes=[pltpu.VMEM((slots,) + rest, jnp.float32)]
        + [pltpu.VMEM(out.shape, out.dtype) for out in outs]
        + [pltpu.SemaphoreType.DMA((slots,)), pltpu.SemaphoreType.DMA((1 + 2 * slots,))],
        cost_estimate=pl.CostEstimate(flops=6 * half * rows_grad.size, bytes_accessed=4 << 20, transcendentals=0),
        compiler_params=pltpu.CompilerParams(vmem_limit_bytes=56 << 20),
        name="front",
    )(core.reshape(1), block_ids, counts, group_map, coef, ids, rows_grad, cold_table)


def adagrad_kernel(place_ref, grad_ref, weights_ref, accum_ref, *refs):
    new_weights_ref, new_accum_ref = refs[-2:]
    for block in range(8):
        rows = slice(block * 128, (block + 1) * 128)
        grad = grad_ref[rows, :]
        mean = jnp.mean(grad * grad, axis=1, keepdims=True)
        accum = jnp.transpose(jnp.broadcast_to(accum_ref[block : block + 1, :], (128, 128)))
        new_accum = accum + mean
        new_weights_ref[rows, :] = weights_ref[rows, :] - 0.5 * grad / (jnp.sqrt(new_accum) + 1e-06)
        new_accum_ref[block : block + 1, :] = jnp.transpose(new_accum)[:1, :]


def adagrad_half(place, grad, weights, accum, before=None):
    half, width = grad.shape
    at = lambda i, place: (place[0], 0)
    given = () if before is None else tuple(before)
    return pl.pallas_call(
        adagrad_kernel,
        grid_spec=pltpu.PrefetchScalarGridSpec(
            num_scalar_prefetch=1,
            grid=(1,),
            in_specs=[
                pl.BlockSpec((half, width), lambda i, place: (0, 0)),
                pl.BlockSpec((half, width), at),
                pl.BlockSpec((half // width, width), at),
            ]
            + [pl.BlockSpec(memory_space=pl.ANY)] * len(given),
            out_specs=[pl.BlockSpec((half, width), at), pl.BlockSpec((half // width, width), at)],
        ),
        out_shape=[jax.ShapeDtypeStruct(weights.shape, jnp.float32), jax.ShapeDtypeStruct(accum.shape, jnp.float32)],
        input_output_aliases={4: 0, 5: 1} if given else {},
        cost_estimate=pl.CostEstimate(flops=8 * half * width, bytes_accessed=12 * half * width, transcendentals=half * width),
        compiler_params=pltpu.CompilerParams(vmem_limit_bytes=24 << 20),
        name="hot_rows_adagrad",
    )(place.reshape(1), grad, weights, accum, *given)


def shards(cold_table, block_ids, counts, group_map, coef, batch_ids, out_grad, hot_weights, accum):
    slot_count = block_ids.shape[2]
    block_rows = cold_table.shape[3]
    width = cold_table.shape[4]
    hot_rows = hot_weights.shape[0]
    part_rows = block_rows // 8
    core = lax.axis_index("core")

    half = hot_rows // 2
    ids, rows_grad = batch_ids[0], out_grad[0, 0]
    table = cold_table[0, 0].reshape(-1, 4, 2, part_rows, width)
    theirs, parity, away = front(core, block_ids, counts, group_map, coef, ids, rows_grad, table, half)
    arrived = swap(theirs, "core")
    grad = added(own_half(core, ids, rows_grad, half), arrived)
    away, grad = lax.optimization_barrier((away, grad))
    parity = parity + swap(away, "core")
    parity = parity.reshape(2, slot_count, 2, 2, part_rows, width)
    near_y, far_y = lax.axis_index("yl"), lax.axis_index("ym")
    send_near = pick(parity, 1 - near_y, 3)
    parity = pick(parity, near_y, 3) + swap(send_near, "yl")
    send_far = pick(parity, 1 - far_y, 2)
    mine, last = pick(parity, far_y, 2), swap(send_far, "ym")

    near = size(NEAR)
    parts = exchange(grad.reshape(near, half // near, width), NEAR)
    parts = exchange(sum_copies(parts, size(FAR), send_near), FAR)
    grad = exchange(sum_copies(parts, near, send_far), NEAR).reshape(half, width)
    grad, parity_shards = lax.optimization_barrier((grad, (mine + last)[None, None]))
    other = swap(grad, "core")
    sums = accum.reshape(hot_rows // width, width)
    done = adagrad_half(core, grad, hot_weights, sums)
    new_weights, new_accum = adagrad_half(1 - core, other, hot_weights, sums, done)
    new_accum = new_accum.reshape(hot_rows)
    return (parity_shards, new_weights, new_accum)


def solution(mesh):
    mesh = Mesh(mesh.devices.reshape(SIZES), NAMES)
    in_specs = (
        P(CODE, DP, None, None, None),
        P(CODE, DP, None),
        P(CODE, DP),
        P(CODE),
        P(),
        P(CODE, DP, None),
        P(CODE, DP, None, None),
        P(),
        P(),
    )
    out_specs = (P(CODE, DP, None, None, None, None), P(), P())
    return jax.shard_map(shards, mesh=mesh, in_specs=in_specs, out_specs=out_specs, check_vma=False)
```
